256 devices in a mesh: replica: 2 (over x_lo), head: 8 (over z), blk: 16 (over y, x_hi, core).
Axes of the slice: x: 4 (x_hi: 2, x_lo: 2; x = x_hi * 2 + x_lo), y: 4, z: 8, core: 2. Of those that a mesh axis runs over, the one named last changes fastest.
Arguments:
- nodes: float32 [65536, 512], P(('replica', 'blk'))
- w_query: float32 [512, 512], P(None, 'head'), may hold values from -0.25 to 0.25
- w_key: float32 [512, 512], P(None, 'head'), may hold values from -0.25 to 0.25
- w_value: float32 [512, 512], P(None, 'head'), may hold values from -0.25 to 0.25
- w_out: float32 [512, 512], P('head'), may hold values from -0.25 to 0.25
- tile_cols: int32 [256, 4], P(('replica', 'blk')), may hold values from 0 to 255, as said below
- tile_masks: int32 [256, 4, 256, 256], P(('replica', 'blk')), may hold values 0 or 1
Outputs:
- updated: float32 [65536, 512], P(('replica', 'blk'), 'head')
- log_sums: float32 [65536, 8], P(('replica', 'blk'), 'head')
The draws below stay inside these ranges and needn't reach their ends.
Inputs may be any that keep to these rules, and one draw needn't show every extreme that they name: `tile_cols`: entry 0 of row a is a; the 4 entries of a row are distinct.
All inputs are finite; a program needn't handle non-finite values. No bound on the sum of `tile_masks` on one device may be relied on, other than what follows from the above.
Results may differ from the reference program's by a relative error of at most 0.0003.
Values sent between devices are 32-bit elements; how exact they have to be, the bound alone decides.
A program may use at most 192 MiB of HBM per device.

```python
import jax
import jax.numpy as jnp
from jax import lax

D = 512
HEADS = 8
HD = 64
BLOCK = 256
TILES = 4
NBLK_ALL = 256
NODES = 65536


def draw_nodes(key, part):
    key = jax.random.fold_in(key, 5)
    first_key = jax.random.fold_in(key, 0)
    return jax.random.normal(first_key, (NODES, D), jnp.float32)


def draw_tile_cols(key, part):
    key = jax.random.fold_in(key, 11)
    row_keys = jax.random.split(key, NBLK_ALL)

    def one_row(row_key, row_index):
        others = jax.random.permutation(row_key, NBLK_ALL - 1)[:TILES - 1].astype(jnp.int32)
        others = others + (others >= row_index).astype(jnp.int32)
        return jnp.concatenate([row_index[None], others]).astype(jnp.int32)
    return jax.vmap(one_row)(row_keys, jnp.arange(NBLK_ALL, dtype=jnp.int32))


def with_ends(values, rng, low, largest):
    longest = values.shape.index(max(values.shape))
    spots = []
    for shift in (0, 1):
        where = [jax.random.randint(jax.random.fold_in(rng, axis), (), 0, length) for axis, length in enumerate(values.shape)]
        where[longest] = (where[longest] + shift) % values.shape[longest]
        spots.append(tuple(where))
    return values.at[spots[0]].set(low).at[spots[1]].set(largest)


def block_levels(own_key, dims, pieces, smallest, high):
    def one(position, parts):
        draws = jax.random.uniform(jax.random.fold_in(jax.random.fold_in(own_key, 6), position), (parts,), jnp.float32, smallest / len(pieces), high / len(pieces))
        return jnp.repeat(jnp.exp(draws), dims[position] // parts).reshape((-1,) + (1,) * (len(dims) - position - 1))

    factor_of = one(*pieces[0])
    for cut in pieces[1:]:
        factor_of = factor_of * one(*cut)
    return factor_of


def scatter_about(rng, extent, scale, limit, cuts=(), held_as=jnp.bfloat16):
    array = jax.random.normal(rng, extent, jnp.float32) * scale
    if len(cuts) > 0:
        array = block_levels(rng, extent, cuts, -0.22, 0.18) * array
    return jnp.clip(array, min=-limit, max=limit).astype(held_as)


def setup_inputs(seed: int = 0) -> dict:
    key_of = jax.random.split(jax.random.key(seed), 8)
    return {
        "nodes": draw_nodes(jax.random.fold_in(key_of[7], 71), 0),
        "w_query": scatter_about(key_of[1], (D, D), D ** -0.5, 0.25, ((1, 8),), jnp.float32),
        "w_key": scatter_about(key_of[2], (D, D), D ** -0.5, 0.25, ((1, 8),), jnp.float32),
        "w_value": scatter_about(key_of[3], (D, D), D ** -0.5, 0.25, ((1, 8),), jnp.float32),
        "w_out": scatter_about(key_of[4], (D, D), D ** -0.5, 0.25, ((0, 8),), jnp.float32),
        "tile_cols": draw_tile_cols(jax.random.fold_in(key_of[7], 71), 0),
        "tile_masks": with_ends((jax.random.randint(key_of[6], (NBLK_ALL, TILES, BLOCK, BLOCK), 0, 8) < 1).astype(jnp.int32), jax.random.fold_in(key_of[6], 1), 0, 1),
    }


def edge_table(tile_masks):
    count_rows = tile_masks.shape[2]
    eye_table = jnp.eye(count_rows, dtype=jnp.float32)
    first_tile = (jnp.arange(tile_masks.shape[1]) == 0).astype(jnp.float32)
    return jnp.maximum(tile_masks.astype(jnp.float32), first_tile[None, :, None, None] * eye_table[None, None])


def reference(nodes, w_query, w_key, w_value, w_out, tile_cols, tile_masks):
    highest = lax.Precision.HIGHEST
    queries = jnp.dot(nodes, w_query, precision=highest, preferred_element_type=jnp.float32).reshape(NBLK_ALL, BLOCK, HEADS, HD)
    keys_all = jnp.dot(nodes, w_key, precision=highest, preferred_element_type=jnp.float32).reshape(NBLK_ALL, BLOCK, HEADS, HD)
    values_all = jnp.dot(nodes, w_value, precision=highest, preferred_element_type=jnp.float32).reshape(NBLK_ALL, BLOCK, HEADS, HD)
    live = edge_table(tile_masks) > 0.5
    score_scale = 1.0 / (HD ** 0.5)

    def one_head(head_index):
        query_head = queries[:, :, head_index, :]
        key_head = keys_all[:, :, head_index, :][tile_cols]
        value_head = values_all[:, :, head_index, :][tile_cols]
        scores = jnp.einsum("bid,btjd->btij", query_head, key_head, precision=highest) * score_scale
        scores = jnp.where(live, scores, -1e30)
        top_score = jnp.max(scores, axis=(1, 3))
        weights = jnp.where(live, jnp.exp(scores - top_score[:, None, :, None]), 0.0)
        totals = jnp.sum(weights, axis=(1, 3))
        attended = jnp.einsum("btij,btjd->bid", weights, value_head, precision=highest) / totals[:, :, None]
        return attended.reshape(NODES, HD), (top_score + jnp.log(totals)).reshape(NODES)

    attended_all, log_all = lax.map(one_head, jnp.arange(HEADS, dtype=jnp.int32))
    merged = attended_all.transpose(1, 0, 2).reshape(NODES, HEADS * HD)
    updated = nodes + jnp.dot(merged, w_out, precision=highest, preferred_element_type=jnp.float32)
    return updated, log_all.T
```

```python
import functools

import jax
import jax.numpy as jnp
from jax import lax
from jax.experimental import pallas as pl
from jax.experimental.pallas import tpu as pltpu
from jax.sharding import PartitionSpec as P

MESH = pl.DeviceIdType.MESH
F32 = jnp.float32
BF16 = jnp.bfloat16

HEADS = 8
HD = 64
BLOCK = 256
HALF = 128
TILES = 4
OWN = 8
CHIP = 16
RING = 4
GROUP = RING * CHIP


def place():
    replica, blk = lax.axis_index("replica"), lax.axis_index("blk")
    core = lax.rem(blk, 2)
    x = lax.rem(lax.div(blk, 2), 2) * 2 + replica
    y = lax.div(blk, 4)
    return x, y, core


def device(x, y, core):
    return {"replica": lax.rem(x, 2), "blk": (y * 2 + lax.div(x, 2)) * 2 + core}


def split(value):
    high = value.astype(BF16).astype(F32)
    return high, value - high


def turned(value):
    return pltpu.roll(value, HD, 1)


def first_lanes(shape):
    return lax.broadcasted_iota(jnp.int32, shape, 1) < HD


def greet(devices):
    barrier = pltpu.get_barrier_semaphore()
    for one in devices:
        pl.semaphore_signal(barrier, inc=1, device_id=one, device_id_type=MESH)
    pl.semaphore_wait(barrier, len(devices))


def remote(src, dst, send, recv, to):
    return pltpu.make_async_remote_copy(
        src_ref=src, dst_ref=dst, send_sem=send, recv_sem=recv, device_id=to, device_id_type=MESH
    )


def project_kernel(nodes, w, grp, qcat, mine, ring_send, ring_recv, pass_send, pass_recv, sib_send, sib_recv):
    x, y, core = place()
    other = 1 - core
    sibling = device(x, y, other)

    def along(step):
        return device(lax.rem(x + step * other, RING), lax.rem(y + step * core, RING), core)

    here = x * other + y * core
    before, after = lax.rem(here + RING - 1, RING), lax.rem(here + 1, RING)
    greet([sibling, along(1), along(RING - 1)])

    w_high, w_low = split(w[...])
    w_high, w_low = w_high.astype(BF16), w_low.astype(BF16)

    @pl.loop(0, OWN)
    def _(i):
        rows = pl.ds(pl.multiple_of(i * BLOCK, BLOCK), BLOCK)
        high, low = split(nodes[rows, :])
        high, low = high.astype(BF16), low.astype(BF16)
        out = (
            jnp.dot(high, w_high, preferred_element_type=F32)
            + jnp.dot(high, w_low, preferred_element_type=F32)
            + jnp.dot(low, w_high, preferred_element_type=F32)
        )
        mine[0, i] = out[:HALF, :HALF]
        mine[1, i] = out[HALF:, :HALF]
        query = out[:, HALF:] * (1.0 / HD**0.5)
        q_high, q_low = split(query)
        qcat[rows, :HALF] = q_high.astype(BF16)
        qcat[rows, HALF:] = q_low.astype(BF16)

    def part(position, chunk):
        return grp.at[pl.ds(position * CHIP + chunk * OWN, OWN)]

    there = x * core + y * other
    to_sibling = remote(mine.at[other], part(there, core), sib_send, sib_recv, sibling)
    to_sibling.start()
    sends = []
    for way, step in enumerate((1, RING - 1)):
        send = remote(mine.at[core], part(here, core), ring_send.at[way, 0], ring_recv.at[way, 0], along(step))
        send.start()
        sends.append(send)

    @pl.loop(0, OWN)
    def _(i):
        grp[here * CHIP + core * OWN + i] = mine[core, i]

    to_sibling.wait()
    for way, step in enumerate((1, RING - 1)):
        send = remote(part(here, other), part(here, other), ring_send.at[way, 1], ring_recv.at[way, 1], along(step))
        send.start()
        sends.append(send)
    sends[0].wait_recv()
    on = remote(part(before, core), part(before, core), pass_send.at[0], pass_recv.at[0], along(1))
    on.start()
    sends[1].wait_recv()
    sends[3].wait_recv()
    back = remote(part(after, other), part(after, other), pass_send.at[1], pass_recv.at[1], along(RING - 1))
    back.start()
    sends[2].wait_recv()
    on.wait_recv()
    back.wait_recv()
    for send in sends:
        send.wait_send()
    on.wait_send()
    back.wait_send()


def attend_kernel(
    loc, grp, qcat, nodes, w_out, masks, updated, log_sums,
    big, mask_v, score, node_v, wall, attended, arrived, columns, columns_in,
    mask_sem, node_sem, ring_send, ring_recv, pass_send, pass_recv, sib_send, sib_recv,
    own_send, own_recv, wout_send, wout_recv, a_send, a_recv, b_send, b_recv,
):
    x, y, core = place()
    head = lax.axis_index("head")
    other = 1 - core
    sibling = device(x, y, other)

    def along(step):
        return device(lax.rem(x + step * core, RING), lax.rem(y + step * other, RING), core)

    here = x * core + y * other
    before, after = lax.rem(here + RING - 1, RING), lax.rem(here + 1, RING)

    def peer(step):
        return {"head": lax.rem(head + step, HEADS)}

    mask_copy = pltpu.make_async_copy(masks, mask_v, mask_sem)
    mask_copy.start()
    node_copy = pltpu.make_async_copy(nodes.at[pl.ds(pl.multiple_of(head * BLOCK, BLOCK), BLOCK)], node_v, node_sem)
    node_copy.start()
    greet([sibling, along(1), along(RING - 1)] + [peer(k) for k in range(1, HEADS)])

    def spot(position, p, chunk):
        return big.at[core, pl.ds((position * RING + p) * CHIP + chunk * OWN, OWN)]

    sends = {}
    for p in range(RING):
        for chunk in range(2):
            for way, step in enumerate((1, RING - 1)):
                part = chunk if way == 0 else 1 - chunk
                send = remote(
                    grp.at[pl.ds(p * CHIP + part * OWN, OWN)], spot(here, p, part),
                    ring_send.at[way, p, part], ring_recv.at[way, p, part], along(step),
                )
                send.start()
                sends[way, p, part] = send
    own = remote(grp, big.at[core, pl.ds(here * GROUP, GROUP)], own_send, own_recv, sibling)
    own.start()
    wouts = []
    for k in range(1, HEADS):
        send = remote(w_out, wall.at[head], wout_send.at[k - 1], wout_recv.at[k - 1], peer(k))
        send.start()
        wouts.append(send)
    wall[head] = w_out[...]

    @pl.loop(0, GROUP)
    def _(i):
        big[core, here * GROUP + i] = grp[i]

    forwards = []
    passes = []

    def forward(position, p, chunk, sem):
        send = remote(spot(position, p, chunk), spot(position, p, chunk), sib_send.at[sem], sib_recv.at[sem], sibling)
        send.start()
        forwards.append(send)

    for chunk in range(2):
        for p in range(RING):
            for way in range(2):
                part = chunk if way == 0 else 1 - chunk
                origin = before if way == 0 else after
                sends[way, p, part].wait_recv()
                if chunk == 0:
                    step = 1 if way == 0 else RING - 1
                    send = remote(
                        spot(origin, p, part), spot(origin, p, part), pass_send.at[way, p], pass_recv.at[way, p], along(step)
                    )
                    send.start()
                    passes.append((send, p, part))
                forward(origin, p, part, len(forwards))
    far = lax.rem(here + 2, RING)
    for send, p, part in passes:
        send.wait_recv()
        forward(far, p, part, len(forwards))
    mask_copy.wait()
    own.wait()
    for send in forwards:
        send.wait()
    for send in sends.values():
        send.wait_send()
    for send, _, _ in passes:
        send.wait_send()

    lanes = first_lanes((HALF, HALF))

    def a_copy(offset):
        return remote(
            attended.at[offset], arrived.at[head], a_send.at[offset], a_recv.at[offset], peer(offset)
        )

    @pl.loop(0, OWN)
    def _(s):
        odd = lax.rem(s, 2)
        offset = 4 + lax.div(s, 2) * (1 - odd) - lax.div(s + 1, 2) * odd
        row = lax.rem(head + offset, HEADS)
        rows = pl.ds(pl.multiple_of(row * BLOCK, BLOCK), BLOCK)
        query = qcat[rows, :]
        values = []
        for t in range(TILES):
            for half in range(2):
                kv = big[half, loc[half, row * TILES + t]]
                high, low = split(kv)
                keys = jnp.where(lanes, high, turned(low)).astype(BF16)
                values.append(jnp.where(lanes, turned(high), low).astype(BF16))
                found = lax.dot_general(
                    query, jnp.concatenate([keys, keys], axis=1), (((1,), (1,)), ((), ())), preferred_element_type=F32
                )
                live = mask_v[row, t, :, half * HALF : (half + 1) * HALF] != 0
                if t == 0:
                    i = lax.broadcasted_iota(jnp.int32, (BLOCK, HALF), 0)
                    j = lax.broadcasted_iota(jnp.int32, (BLOCK, HALF), 1) + half * HALF
                    live = live | (i == j)
                n = t * 2 + half
                score[:, n * HALF : (n + 1) * HALF] = jnp.where(live, found, -1e30)
        top = jnp.max(score[...], axis=1, keepdims=True)
        weights = jnp.exp(score[...] - top)
        total = jnp.sum(weights, axis=1, keepdims=True)
        high = weights.astype(BF16)
        low = (weights - high.astype(F32)).astype(BF16)
        value = jnp.concatenate(values, axis=0)
        both = jnp.dot(high, value, preferred_element_type=F32) + jnp.dot(low, value, preferred_element_type=F32)
        result = (both + turned(both)) / total
        log_sums[rows, :] = top + jnp.log(total)
        packed = jnp.where(lanes, result[:HALF], result[HALF:])

        @pl.when(offset != 0)
        def _():
            attended[offset] = packed
            a_copy(offset).start()

        @pl.when(offset == 0)
        def _():
            arrived[head] = packed

    for send in wouts:
        send.wait()
    node_copy.wait()
    for k in range(1, HEADS):
        a_copy(k).wait()
    merged = []
    for pair in range(HEADS // 2):
        one, two = arrived[2 * pair], arrived[2 * pair + 1]
        merged.append(jnp.concatenate([jnp.where(lanes, one, turned(two)), jnp.where(lanes, turned(one), two)], axis=0))
    merged = jnp.concatenate(merged, axis=1)
    m_high, m_low = split(merged)
    m_high, m_low = m_high.astype(BF16), m_low.astype(BF16)
    w_high, w_low = split(wall[...].reshape(HEADS * HD, HEADS * HD))
    w_high, w_low = w_high.astype(BF16), w_low.astype(BF16)
    mixed = node_v[...] + (
        jnp.dot(m_high, w_high, preferred_element_type=F32)
        + jnp.dot(m_high, w_low, preferred_element_type=F32)
        + jnp.dot(m_low, w_high, preferred_element_type=F32)
    )
    for pair in range(HEADS // 2):
        both = mixed[:, pair * HALF : (pair + 1) * HALF]
        up, down = both[:HALF], both[HALF:]
        columns[2 * pair] = jnp.where(lanes, up, turned(down))
        columns[2 * pair + 1] = jnp.where(lanes, turned(up), down)
    finals = []
    for k in range(1, HEADS):
        send = remote(
            columns.at[lax.rem(head + k, HEADS)], columns_in.at[head], b_send.at[k - 1], b_recv.at[k - 1], peer(k)
        )
        send.start()
        finals.append(send)
    columns_in[head] = columns[head]
    for send in finals:
        send.wait()
    for row in range(OWN):
        packed = columns_in[row]
        updated[row * BLOCK : row * BLOCK + HALF, :] = packed[:, :HD]
        updated[row * BLOCK + HALF : (row + 1) * BLOCK, :] = turned(packed)[:, :HD]


def body(nodes, w_query, w_key, w_value, w_out, tile_cols, tile_masks):
    w = jnp.concatenate([w_key, w_value, w_query, w_query], axis=1)
    vmem = pl.BlockSpec(memory_space=pltpu.VMEM)
    smem = pl.BlockSpec(memory_space=pltpu.SMEM)
    hbm = pl.BlockSpec(memory_space=pl.ANY)
    dma = pltpu.SemaphoreType.DMA
    rows = nodes.shape[0]
    grp, qcat = pl.pallas_call(
        project_kernel,
        out_shape=(
            jax.ShapeDtypeStruct((GROUP, HALF, HALF), F32),
            jax.ShapeDtypeStruct((rows, 2 * HALF), BF16),
        ),
        in_specs=[vmem, vmem],
        out_specs=(vmem, vmem),
        scratch_shapes=[
            pltpu.VMEM((2, OWN, HALF, HALF), F32),
            dma((2, 2)), dma((2, 2)), dma((2,)), dma((2,)), dma, dma,
        ],
        compiler_params=pltpu.CompilerParams(
            collective_id=0, has_side_effects=True, vmem_limit_bytes=40 * 2**20
        ),
        name="project",
    )(nodes, w)

    replica, blk, i = tile_cols // 128, (tile_cols // 8) % 16, tile_cols % 8
    x, y, core = (blk // 2) % 2 * 2 + replica, blk // 4, blk % 2
    loc = jnp.stack([(y * RING + x) * CHIP + core * OWN + i, (x * RING + y) * CHIP + core * OWN + i])
    loc = loc.reshape(2, OWN * TILES)
    updated, log_sums = pl.pallas_call(
        attend_kernel,
        out_shape=(
            jax.ShapeDtypeStruct((rows, HD), F32),
            jax.ShapeDtypeStruct((rows, 1), F32),
        ),
        in_specs=[smem, vmem, vmem, hbm, vmem, hbm],
        out_specs=(vmem, vmem),
        scratch_shapes=[
            pltpu.VMEM((2, RING * GROUP, HALF, HALF), F32),
            pltpu.VMEM((OWN, TILES, BLOCK, BLOCK), jnp.int32),
            pltpu.VMEM((BLOCK, TILES * BLOCK), F32),
            pltpu.VMEM((BLOCK, HEADS * HD), F32),
            pltpu.VMEM((HEADS, HD, HEADS * HD), F32),
            pltpu.VMEM((HEADS, HALF, HALF), F32),
            pltpu.VMEM((HEADS, HALF, HALF), F32),
            pltpu.VMEM((HEADS, HALF, HALF), F32),
            pltpu.VMEM((HEADS, HALF, HALF), F32),
            dma, dma,
            dma((2, RING, 2)), dma((2, RING, 2)), dma((2, RING)), dma((2, RING)), dma((24,)), dma((24,)),
            dma, dma, dma((HEADS - 1,)), dma((HEADS - 1,)),
            dma((HEADS,)), dma((HEADS,)), dma((HEADS - 1,)), dma((HEADS - 1,)),
        ],
        compiler_params=pltpu.CompilerParams(
            collective_id=1, has_side_effects=True, vmem_limit_bytes=60 * 2**20
        ),
        name="attend",
    )(loc, grp, qcat, nodes, w_out, tile_masks)
    return updated, log_sums


def solution(mesh):
    placed = (
        P(("replica", "blk"), None),
        P(None, "head"),
        P(None, "head"),
        P(None, "head"),
        P("head", None),
        P(("replica", "blk"), None),
        P(("replica", "blk"), None, None, None),
    )
    return jax.shard_map(
        body,
        mesh=mesh,
        in_specs=placed,
        out_specs=(P(("replica", "blk"), "head"), P(("replica", "blk"), "head")),
        check_vma=False,
    )
```

```python
import jax
import jax.numpy as jnp
from jax import lax
from jax.experimental import pallas as pl
from jax.experimental.pallas import tpu as pltpu
from jax.sharding import PartitionSpec as P

MESH = pl.DeviceIdType.MESH
F32 = jnp.float32
BF16 = jnp.bfloat16
I32 = jnp.int32

HEADS = 8
HD = 64
BLOCK = 256
HALF = 128
TILES = 4
OWN = 8
CHIP = 16
RING = 4
GROUP = RING * CHIP
BLOCKS = RING * GROUP
SLOTS = 22
PART = SLOTS // 2
NEEDS = OWN * TILES
PICK, SPOT, PLACE, MOST = 0, 8, 16, 24


def place():
    replica, blk = lax.axis_index("replica"), lax.axis_index("blk")
    core = lax.rem(blk, 2)
    x = lax.rem(lax.div(blk, 2), 2) * 2 + replica
    y = lax.div(blk, 4)
    return x, y, core


def device(x, y, core):
    return {"replica": lax.rem(x, 2), "blk": (y * 2 + lax.div(x, 2)) * 2 + core}


def first_axis(x, y, core):
    def along(step):
        return device(lax.rem(x + step * (1 - core), RING), lax.rem(y + step * core, RING), core)

    return along, x * (1 - core) + y * core


def second_axis(x, y, core):
    def along(step):
        return device(lax.rem(x + step * core, RING), lax.rem(y + step * (1 - core), RING), core)

    return along, x * core + y * (1 - core)


def peer(step):
    return {"head": lax.rem(lax.axis_index("head") + step, HEADS)}


def split(value):
    high = value.astype(BF16).astype(F32)
    return high, value - high


def turned(value):
    return pltpu.roll(value, HD, 1)


def nt(a, b):
    return lax.dot_general(a, b, (((1,), (1,)), ((), ())), preferred_element_type=F32)


def lane(shape):
    return lax.broadcasted_iota(I32, shape, 1)


def greet(devices):
    barrier = pltpu.get_barrier_semaphore()
    for one in devices:
        pl.semaphore_signal(barrier, inc=1, device_id=one, device_id_type=MESH)
    pl.semaphore_wait(barrier, len(devices))


def remote(src, dst, send, recv, to):
    return pltpu.make_async_remote_copy(
        src_ref=src, dst_ref=dst, send_sem=send, recv_sem=recv, device_id=to, device_id_type=MESH
    )


def started(*what):
    copy = remote(*what)
    copy.start()
    return copy


def project_kernel(
    nodes, wk, wv, wq, w_out, asked, grp, qcat, wall, table,
    mine, asked_in, news, news_in, most, most_in,
    ring_send, ring_recv, pass_send, pass_recv, sib_send, sib_recv, asked_send, asked_recv,
    news_send, news_recv, most_send, most_recv, wout_send, wout_recv, share_send, share_recv,
):
    x, y, core = place()
    head = lax.axis_index("head")
    other = 1 - core
    sibling = device(x, y, other)
    along, here = first_axis(x, y, core)
    across, there = second_axis(x, y, core)
    before, after = lax.rem(here + RING - 1, RING), lax.rem(here + 1, RING)
    steps = (1, 2, 3)
    greet(
        [sibling]
        + [along(k) for k in steps]
        + [across(k) for k in steps]
        + [peer(k) for k in range(1, HEADS)]
    )
    ask = started(asked, asked_in, asked_send, asked_recv, sibling)
    lines = pl.ds(pl.multiple_of(core * (HD // 2), HD // 2), HD // 2)
    wouts = [
        started(w_out.at[lines], wall.at[head, lines], wout_send.at[k], wout_recv.at[k], peer(k)) for k in range(1, HEADS)
    ]
    wall[head] = w_out[...]

    w_high, w_low = split(jnp.concatenate([wk[...], wv[...], wq[...], wq[...]], axis=0))
    w_high, w_low = w_high.astype(BF16), w_low.astype(BF16)

    @pl.loop(0, OWN)
    def _(i):
        rows = pl.ds(pl.multiple_of(i * BLOCK, BLOCK), BLOCK)
        high, low = split(nodes[rows, :])
        high, low = high.astype(BF16), low.astype(BF16)
        out = nt(high, w_high) + nt(high, w_low) + nt(low, w_high)
        mine[0, i] = out[:HALF, :HALF]
        mine[1, i] = out[HALF:, :HALF]
        q_high, q_low = split(out[:, HALF:] * (1.0 / HD**0.5))
        qcat[rows, :HALF] = q_high.astype(BF16)
        qcat[rows, HALF:] = q_low.astype(BF16)

    def part(position, chunk):
        return grp.at[pl.ds(position * CHIP + chunk * OWN, OWN)]

    to_sibling = started(mine.at[other], part(there, core), sib_send, sib_recv, sibling)
    sends = [
        started(mine.at[core], part(here, core), ring_send.at[way, 0], ring_recv.at[way, 0], along(step))
        for way, step in enumerate((1, RING - 1))
    ]

    @pl.loop(0, OWN)
    def _(i):
        grp[here * CHIP + core * OWN + i] = mine[core, i]

    to_sibling.wait()
    sends += [
        started(part(here, other), part(here, other), ring_send.at[way, 1], ring_recv.at[way, 1], along(step))
        for way, step in enumerate((1, RING - 1))
    ]

    ask.wait()
    everything = jnp.concatenate([asked[...], asked_in[...]], axis=0)

    def positions(col):
        replica, blk, i = col >> 7, (col >> 3) & 15, col & 7
        px, py, pc = ((blk >> 1) & 1) * 2 + replica, blk >> 2, blk & 1
        return (py * RING + px) * CHIP + pc * OWN + i, (px * RING + py) * CHIP + pc * OWN + i

    used = []
    for wanted in positions(everything):
        ids = lane((2 * NEEDS, HALF))
        hits = [jnp.where(wanted == ids + n * HALF, 1.0, 0.0) for n in range(BLOCKS // HALF)]
        used.append(jnp.concatenate([jnp.max(one, axis=0, keepdims=True) for one in hits], axis=1))
    line = lax.broadcasted_iota(I32, (8, BLOCKS), 0)
    used = jnp.where(line == 0, used[0], jnp.where(line == 1, used[1], 0.0))
    i, j = lax.broadcasted_iota(I32, (BLOCKS, BLOCKS), 0), lane((BLOCKS, BLOCKS))
    earlier = jnp.where((i < j) & ((i >> 6) == (j >> 6)), 1.0, 0.0).astype(BF16)
    ranks = jnp.dot(used.astype(BF16), earlier, preferred_element_type=F32)
    home = jnp.where(line == 0, y, x)
    filled = jnp.where((used > 0.5) & ((lane((8, BLOCKS)) >> 6) != home), ranks + 1.0, 0.0)
    own_most = jnp.max(jnp.max(filled, axis=0, keepdims=True), axis=1, keepdims=True)
    news[0] = used
    news[1] = ranks
    news[2] = jnp.broadcast_to(own_most, (8, BLOCKS))
    tell = [
        started(news, news_in.at[RING - k], news_send.at[k], news_recv.at[RING - k], across(k)) for k in steps
    ]

    sends[0].wait_recv()
    on = started(part(before, core), part(before, core), pass_send.at[0], pass_recv.at[0], along(1))

    column = lane((NEEDS, HALF))
    result = jnp.zeros((NEEDS, HALF), F32)
    for half, wanted in enumerate(positions(asked[...])):
        rank = jnp.zeros((NEEDS, 1), F32)
        for n in range(BLOCKS // HALF):
            row = ranks[half : half + 1, n * HALF : (n + 1) * HALF]
            rank += jnp.sum(jnp.where(wanted == column + n * HALF, row, 0.0), axis=1, keepdims=True)
        away = ((wanted >> 6) + RING - (y if half == 0 else x)) & 3
        slot = jnp.where(away == 0, (wanted & 63).astype(F32), (GROUP + (away - 1) * SLOTS).astype(F32) + rank)
        result = jnp.where(column == SPOT + half, slot, result)
        result = jnp.where(column == PLACE + half, wanted.astype(F32), result)

    for send in tell:
        send.wait()
    top = news[2]
    for k in steps:
        top = jnp.maximum(top, news_in[k, 2])
    most[...] = top
    tell_most = [
        started(most, most_in.at[RING - k], most_send.at[k], most_recv.at[RING - k], along(k)) for k in steps
    ]
    ids = lane((1, BLOCKS))
    slot = lax.broadcasted_iota(I32, (NEEDS, BLOCKS), 0).astype(F32)
    for k in steps:
        use = jnp.where(core == 0, news_in[k, 0, 0:1, :], news_in[k, 0, 1:2, :])
        rank = jnp.where(core == 0, news_in[k, 1, 0:1, :], news_in[k, 1, 1:2, :])
        rank = jnp.where((use > 0.5) & ((ids >> 6) == there), rank, -1.0)
        pick = jnp.sum(jnp.where(rank == slot, (ids & 63).astype(F32), 0.0), axis=1, keepdims=True)
        result = jnp.where(column == PICK + k, pick, result)

    sends[1].wait_recv()
    sends[3].wait_recv()
    back = started(part(after, other), part(after, other), pass_send.at[1], pass_recv.at[1], along(RING - 1))
    shares = []
    for k in range(1, HEADS):
        wouts[k - 1].wait()
        spot = wall.at[lax.rem(head + HEADS - k, HEADS), lines]
        shares.append(started(spot, spot, share_send.at[k], share_recv.at[k], sibling))
    for send in tell_most:
        send.wait()
    for k in steps:
        top = jnp.maximum(top, most_in[k])
    top = jnp.max(top[:, :HALF], axis=0, keepdims=True)
    result = jnp.where(column == MOST, top, result)
    table[...] = result.astype(I32)

    sends[2].wait_recv()
    on.wait_recv()
    back.wait_recv()
    for send in shares:
        send.wait()
    for send in sends:
        send.wait_send()
    on.wait_send()
    back.wait_send()


def prepare(nodes_v, wall, w_high, w_low, nodes_t):
    high, low = split(wall[...].reshape(HEADS * HD, HEADS * HD).T)
    w_high[...] = high.astype(BF16)
    w_low[...] = low.astype(BF16)
    nodes_t[...] = nodes_v[...].T


def finish(
    table, base, qcat, updated, log_sums, held, mask_v, w_high, w_low, nodes_t,
    score, sums, attended, arrived, columns, a_send, a_recv, b_send, b_recv,
):
    head = lax.axis_index("head")
    lanes = lane((HALF, HALF)) < HD

    def a_copy(offset):
        return remote(attended.at[offset], arrived.at[head], a_send.at[offset], a_recv.at[offset], peer(offset))

    @pl.loop(0, OWN)
    def _(s):
        odd = lax.rem(s, 2)
        offset = 4 + lax.div(s, 2) * (1 - odd) - lax.div(s + 1, 2) * odd
        row = lax.rem(head + offset, HEADS)
        rows = pl.ds(pl.multiple_of(row * BLOCK, BLOCK), BLOCK)
        query = qcat[rows, :]
        values = []
        for t in range(TILES):
            for half in range(2):
                high, low = split(held[half, table[row * TILES + t, base + half]])
                keys = jnp.where(lanes, high, turned(low)).astype(BF16)
                values.append(jnp.where(lanes, turned(high), low).astype(BF16))
                found = nt(query, jnp.concatenate([keys, keys], axis=1))
                live = mask_v[row, t, :, half * HALF : (half + 1) * HALF] != 0
                if t == 0:
                    i = lax.broadcasted_iota(I32, (BLOCK, HALF), 0)
                    live = live | (i == lane((BLOCK, HALF)) + half * HALF)
                n = t * 2 + half
                score[:, n * HALF : (n + 1) * HALF] = jnp.where(live, found, -1e30)
        top = jnp.max(score[...], axis=1, keepdims=True)
        weights = jnp.exp(score[...] - top)
        total = jnp.sum(weights, axis=1, keepdims=True)
        high = weights.astype(BF16)
        low = (weights - high.astype(F32)).astype(BF16)
        value = jnp.concatenate(values, axis=0)
        both = jnp.dot(high, value, preferred_element_type=F32) + jnp.dot(low, value, preferred_element_type=F32)
        result = (both + turned(both)) / total
        sums[...] = jnp.where(lane((BLOCK, HALF)) == row, top + jnp.log(total), sums[...])
        packed = jnp.where(lanes, result[:HALF], result[HALF:])

        @pl.when(offset != 0)
        def _():
            attended[offset] = packed
            a_copy(offset).start()

        @pl.when(offset == 0)
        def _():
            arrived[head] = packed

    for k in range(1, HEADS):
        a_copy(k).wait()
    merged = []
    for pair in range(HEADS // 2):
        one, two = arrived[2 * pair], arrived[2 * pair + 1]
        merged.append(jnp.concatenate([jnp.where(lanes, one, turned(two)), jnp.where(lanes, turned(one), two)], axis=0))
    m_high, m_low = split(jnp.concatenate(merged, axis=1))
    m_high, m_low = m_high.astype(BF16), m_low.astype(BF16)
    columns[...] = nodes_t[...] + (nt(w_high[...], m_high) + nt(w_low[...], m_high) + nt(w_high[...], m_low))
    mine = pl.ds(pl.multiple_of(head * BLOCK, BLOCK), BLOCK)
    finals = []
    for k in range(1, HEADS):
        rows = pl.ds(pl.multiple_of(lax.rem(head + k, HEADS) * HD, HD), HD)
        finals.append(started(columns.at[rows], updated.at[:, mine], b_send.at[k], b_recv.at[k], peer(k)))
    updated[:, mine] = columns[pl.ds(pl.multiple_of(head * HD, HD), HD), :]
    flat = sums[...].T
    for row in range(OWN):
        log_sums[:, row * BLOCK : (row + 1) * BLOCK] = flat[row : row + 1, :]
    for send in finals:
        send.wait()


def fetch(nodes, masks, node_v, mask_v, node_sem, mask_sem):
    start = pl.multiple_of(lax.axis_index("head") * BLOCK, BLOCK)
    node_copy = pltpu.make_async_copy(nodes.at[pl.ds(start, BLOCK)], node_v, node_sem)
    node_copy.start()
    mask_copy = pltpu.make_async_copy(masks, mask_v, mask_sem)
    mask_copy.start()
    return node_copy, mask_copy


def picked_kernel(
    table, grp, qcat, wall, nodes, masks, updated, log_sums,
    held, packets, relay, mask_v, node_v, w_high, w_low, nodes_t, score, sums, attended, arrived, columns,
    mask_sem, node_sem, own_send, own_recv, ring_send, ring_recv, far_send, far_recv, pass_send, pass_recv,
    sib_send, sib_recv, a_send, a_recv, b_send, b_recv,
):
    x, y, core = place()
    sibling = device(x, y, 1 - core)
    along, _ = second_axis(x, y, core)
    ways = (1, RING - 1)
    node_copy, mask_copy = fetch(nodes, masks, node_v, mask_v, node_sem, mask_sem)

    def fill(k):
        @pl.loop(0, SLOTS)
        def _(s):
            packets[k, s] = grp[table[s, PICK + k]]

    def spot(away, chunk):
        return held.at[core, pl.ds(GROUP + (away - 1) * SLOTS + chunk * PART, PART)]

    fill(2)
    greet([sibling, along(1), along(RING - 1)] + [peer(k) for k in range(1, HEADS)])
    fars = [
        started(packets.at[2, pl.ds(way * PART, PART)], relay.at[way], far_send.at[way], far_recv.at[way], along(step))
        for way, step in enumerate(ways)
    ]
    sends = []
    for step in ways:
        fill(step)
    for chunk in range(2):
        for way, step in enumerate(ways):
            sends.append(started(
                packets.at[step, pl.ds(chunk * PART, PART)], spot(RING - step, chunk),
                ring_send.at[way, chunk], ring_recv.at[way, chunk], along(step),
            ))
    own = started(grp, held.at[core, pl.ds(0, GROUP)], own_send, own_recv, sibling)

    @pl.loop(0, GROUP)
    def _(i):
        held[core, i] = grp[i]

    sums[...] = jnp.zeros_like(sums)
    node_copy.wait()
    prepare(node_v, wall, w_high, w_low, nodes_t)

    passes = []
    for way, step in enumerate(ways):
        fars[way].wait_recv()
        passes.append(started(relay.at[way], spot(2, way), pass_send.at[way], pass_recv.at[way], along(step)))
    forwards = []

    def forward(away, chunk):
        n = len(forwards)
        forwards.append(started(spot(away, chunk), spot(away, chunk), sib_send.at[n], sib_recv.at[n], sibling))

    for n, send in enumerate(sends):
        send.wait_recv()
        forward(RING - ways[n % 2], n // 2)
    for way in range(2):
        passes[way].wait_recv()
        forward(2, way)
    mask_copy.wait()
    own.wait()
    for send in forwards:
        send.wait()
    for send in fars + sends + passes:
        send.wait_send()
    finish(
        table, SPOT, qcat, updated, log_sums, held, mask_v, w_high, w_low, nodes_t,
        score, sums, attended, arrived, columns, a_send, a_recv, b_send, b_recv,
    )


def whole_kernel(
    table, grp, qcat, wall, nodes, masks, updated, log_sums,
    held, mask_v, node_v, w_high, w_low, nodes_t, score, sums, attended, arrived, columns,
    mask_sem, node_sem, own_send, own_recv, ring_send, ring_recv, pass_send, pass_recv,
    sib_send, sib_recv, a_send, a_recv, b_send, b_recv,
):
    x, y, core = place()
    sibling = device(x, y, 1 - core)
    along, here = second_axis(x, y, core)
    before, after, far = (lax.rem(here + k, RING) for k in (RING - 1, 1, 2))
    ways = (1, RING - 1)
    node_copy, mask_copy = fetch(nodes, masks, node_v, mask_v, node_sem, mask_sem)
    greet([sibling, along(1), along(RING - 1)] + [peer(k) for k in range(1, HEADS)])

    def spot(position, p, chunk):
        return held.at[core, pl.ds((position * RING + p) * CHIP + chunk * OWN, OWN)]

    sends = {}
    for p in range(RING):
        for chunk in range(2):
            for way, step in enumerate(ways):
                part = chunk if way == 0 else 1 - chunk
                sends[way, p, part] = started(
                    grp.at[pl.ds(p * CHIP + part * OWN, OWN)], spot(here, p, part),
                    ring_send.at[way, p, part], ring_recv.at[way, p, part], along(step),
                )
    own = started(grp, held.at[core, pl.ds(here * GROUP, GROUP)], own_send, own_recv, sibling)

    @pl.loop(0, GROUP)
    def _(i):
        held[core, here * GROUP + i] = grp[i]

    sums[...] = jnp.zeros_like(sums)
    node_copy.wait()
    prepare(node_v, wall, w_high, w_low, nodes_t)
    forwards = []
    passes = []

    def forward(position, p, chunk):
        n = len(forwards)
        one = spot(position, p, chunk)
        forwards.append(started(one, one, sib_send.at[n], sib_recv.at[n], sibling))

    for chunk in range(2):
        for p in range(RING):
            for way, step in enumerate(ways):
                part = chunk if way == 0 else 1 - chunk
                origin = before if way == 0 else after
                sends[way, p, part].wait_recv()
                if chunk == 0:
                    one = spot(origin, p, part)
                    passes.append((started(one, one, pass_send.at[way, p], pass_recv.at[way, p], along(step)), p, part))
                forward(origin, p, part)
    for send, p, part in passes:
        send.wait_recv()
        forward(far, p, part)
    mask_copy.wait()
    own.wait()
    for send in forwards:
        send.wait()
    for send in sends.values():
        send.wait_send()
    for send, _, _ in passes:
        send.wait_send()
    finish(
        table, PLACE, qcat, updated, log_sums, held, mask_v, w_high, w_low, nodes_t,
        score, sums, attended, arrived, columns, a_send, a_recv, b_send, b_recv,
    )


def body(nodes, w_query, w_key, w_value, w_out, tile_cols, tile_masks):
    vmem = pl.BlockSpec(memory_space=pltpu.VMEM)
    smem = pl.BlockSpec(memory_space=pltpu.SMEM)
    hbm = pl.BlockSpec(memory_space=pl.ANY)
    dma = pltpu.SemaphoreType.DMA
    rows = nodes.shape[0]
    scratch = pltpu.VMEM
    asked = jnp.broadcast_to(tile_cols.reshape(NEEDS, 1), (NEEDS, HALF))
    grp, qcat, wall, table = pl.pallas_call(
        project_kernel,
        out_shape=(
            jax.ShapeDtypeStruct((GROUP, HALF, HALF), F32),
            jax.ShapeDtypeStruct((rows, 2 * HALF), BF16),
            jax.ShapeDtypeStruct((HEADS, HD, HEADS * HD), F32),
            jax.ShapeDtypeStruct((NEEDS, HALF), I32),
        ),
        in_specs=[vmem] * 6,
        out_specs=(vmem,) * 4,
        scratch_shapes=[
            scratch((2, OWN, HALF, HALF), F32),
            scratch((NEEDS, HALF), I32),
            scratch((3, 8, BLOCKS), F32), scratch((RING, 3, 8, BLOCKS), F32),
            scratch((8, BLOCKS), F32), scratch((RING, 8, BLOCKS), F32),
            dma((2, 2)), dma((2, 2)), dma((2,)), dma((2,)), dma, dma, dma, dma,
            dma((RING,)), dma((RING,)), dma((RING,)), dma((RING,)),
            dma((HEADS,)), dma((HEADS,)), dma((HEADS,)), dma((HEADS,)),
        ],
        compiler_params=pltpu.CompilerParams(collective_id=0, has_side_effects=True, vmem_limit_bytes=24 * 2**20),
        name="project",
    )(nodes, w_key.T, w_value.T, w_query.T, w_out, asked)

    def second(kernel, name, number, slots, extra, semaphores, limit):
        def call(*operands):
            return pl.pallas_call(
                kernel,
                out_shape=(jax.ShapeDtypeStruct((HD, rows), F32), jax.ShapeDtypeStruct((1, rows), F32)),
                in_specs=[smem, vmem, vmem, vmem, hbm, hbm],
                out_specs=(vmem, vmem),
                scratch_shapes=[
                    scratch((2, slots, HALF, HALF), F32),
                    *extra,
                    scratch((OWN, TILES, BLOCK, BLOCK), I32),
                    scratch((BLOCK, HEADS * HD), F32),
                    scratch((HEADS * HD, HEADS * HD), BF16), scratch((HEADS * HD, HEADS * HD), BF16),
                    scratch((HEADS * HD, BLOCK), F32),
                    scratch((BLOCK, TILES * BLOCK), F32),
                    scratch((BLOCK, HALF), F32),
                    scratch((HEADS, HALF, HALF), F32), scratch((HEADS, HALF, HALF), F32),
                    scratch((HEADS * HD, BLOCK), F32),
                    dma, dma, dma, dma,
                    *semaphores,
                    dma((HEADS,)), dma((HEADS,)), dma((HEADS,)), dma((HEADS,)),
                ],
                compiler_params=pltpu.CompilerParams(
                    collective_id=number, has_side_effects=True, vmem_limit_bytes=limit * 2**20
                ),
                name=name,
            )(*operands)

        return call

    picked = second(
        picked_kernel, "picked", 1, GROUP + 3 * SLOTS,
        [scratch((RING, SLOTS, HALF, HALF), F32), scratch((2, PART, HALF, HALF), F32)],
        [dma((2, 2)), dma((2, 2)), dma((2,)), dma((2,)), dma((2,)), dma((2,)), dma((6,)), dma((6,))],
        48,
    )
    whole = second(
        whole_kernel, "whole", 2, BLOCKS, [],
        [dma((2, RING, 2)), dma((2, RING, 2)), dma((2, RING)), dma((2, RING)), dma((24,)), dma((24,))],
        60,
    )
    updated, log_sums = lax.cond(
        table[0, MOST] > SLOTS, whole, picked, table, grp, qcat, wall, nodes, tile_masks
    )
    return updated.T, log_sums.T


def solution(mesh):
    placed = (
        P(("replica", "blk"), None),
        P(None, "head"),
        P(None, "head"),
        P(None, "head"),
        P("head", None),
        P(("replica", "blk"), None),
        P(("replica", "blk"), None, None, None),
    )
    return jax.shard_map(
        body,
        mesh=mesh,
        in_specs=placed,
        out_specs=(P(("replica", "blk"), "head"), P(("replica", "blk"), "head")),
        check_vma=False,
    )
```

```python
import functools

import jax
import jax.numpy as jnp
from jax import lax
from jax.experimental import pallas as pl
from jax.experimental.pallas import tpu as pltpu
from jax.sharding import PartitionSpec as P

MESH = pl.DeviceIdType.MESH
F32 = jnp.float32
BF16 = jnp.bfloat16
I32 = jnp.int32

HEADS = 8
HD = 64
BLOCK = 256
HALF = 128
TILES = 4
OWN = 8
CHIP = 16
RING = 4
GROUP = RING * CHIP
BLOCKS = RING * GROUP
SLOTS = (18, 20, 24)
STRIDE = SLOTS[-1]
NEEDS = OWN * TILES
PICK, SPOT, PLACE, LEVEL = 0, 8, 16, 24


def place():
    replica, blk = lax.axis_index("replica"), lax.axis_index("blk")
    core = lax.rem(blk, 2)
    x = lax.rem(lax.div(blk, 2), 2) * 2 + replica
    y = lax.div(blk, 4)
    return x, y, core


def device(x, y, core):
    return {"replica": lax.rem(x, 2), "blk": (y * 2 + lax.div(x, 2)) * 2 + core}


def first_axis(x, y, core):
    def along(step):
        return device(lax.rem(x + step * (1 - core), RING), lax.rem(y + step * core, RING), core)

    return along, x * (1 - core) + y * core


def second_axis(x, y, core):
    def along(step):
        return device(lax.rem(x + step * core, RING), lax.rem(y + step * (1 - core), RING), core)

    return along, x * core + y * (1 - core)


def peer(step):
    return {"head": lax.rem(lax.axis_index("head") + step, HEADS)}


def split(value):
    high = value.astype(BF16).astype(F32)
    return high, value - high


def turned(value):
    return pltpu.roll(value, HD, 1)


def nt(a, b):
    return lax.dot_general(a, b, (((1,), (1,)), ((), ())), preferred_element_type=F32)


def lane(shape):
    return lax.broadcasted_iota(I32, shape, 1)


def greet(devices):
    for one in devices:
        pl.semaphore_signal(pltpu.get_barrier_semaphore(), inc=1, device_id=one, device_id_type=MESH)


def met(count):
    pl.semaphore_wait(pltpu.get_barrier_semaphore(), count)


def remote(src, dst, send, recv, to):
    return pltpu.make_async_remote_copy(
        src_ref=src, dst_ref=dst, send_sem=send, recv_sem=recv, device_id=to, device_id_type=MESH
    )


def started(*what):
    copy = remote(*what)
    copy.start()
    return copy


def project_kernel(
    nodes, weights, asked, grp, qcat, wall, table,
    nodes_v, w_v, mine, news, news_in, most, most_in,
    node_sem, w_sem, ring_send, ring_recv, pass_send, pass_recv, sib_send, sib_recv,
    news_send, news_recv, most_send, most_recv, wout_send, wout_recv, share_send, share_recv,
):
    x, y, core = place()
    head = lax.axis_index("head")
    other = 1 - core
    sibling = device(x, y, other)
    along, here = first_axis(x, y, core)
    across, there = second_axis(x, y, core)
    sibling_across, _ = second_axis(x, y, other)
    sibling_along, _ = first_axis(x, y, other)
    before, after = lax.rem(here + RING - 1, RING), lax.rem(here + 1, RING)
    steps = (1, 2, 3)
    friends = [sibling] + [peer(k) for k in range(1, HEADS)]
    for ring in (along, across, sibling_across, sibling_along):
        friends += [ring(k) for k in steps]
    greet(friends)
    w_copies = [
        pltpu.make_async_copy(weights.at[pl.ds(0, 3 * HD)], w_v.at[pl.ds(0, 3 * HD)], w_sem.at[0]),
        pltpu.make_async_copy(weights.at[pl.ds(2 * HD, HD)], w_v.at[pl.ds(3 * HD, HD)], w_sem.at[1]),
    ]
    for copy in w_copies:
        copy.start()

    def node_copy(i):
        rows = pl.ds(pl.multiple_of(i * BLOCK, BLOCK), BLOCK)
        return pltpu.make_async_copy(nodes.at[rows], nodes_v.at[rows], node_sem.at[i])

    for i in range(OWN):
        node_copy(i).start()
    wout_copy = pltpu.make_async_copy(weights.at[pl.ds(3 * HD, HD)], wall.at[head], w_sem.at[2])
    wout_copy.start()

    def positions(col):
        replica, blk, i = col >> 7, (col >> 3) & 15, col & 7
        px, py, pc = ((blk >> 1) & 1) * 2 + replica, blk >> 2, blk & 1
        return (py * RING + px) * CHIP + pc * OWN + i, (px * RING + py) * CHIP + pc * OWN + i

    column = lane((NEEDS, HALF))
    wanted = positions(asked[...])
    line = lax.broadcasted_iota(I32, (8, BLOCKS), 0)
    used = jnp.zeros((8, BLOCKS), F32)
    for half in range(2):
        hits = [jnp.where(wanted[half] == column + n * HALF, 1.0, 0.0) for n in range(BLOCKS // HALF)]
        row = jnp.concatenate([jnp.max(one, axis=0, keepdims=True) for one in hits], axis=1)
        used = jnp.where(line == half, row, used)
    news[...] = used
    met(len(friends))
    tells = [started(news, news_in.at[0, core], news_send.at[0, 0], news_recv.at[0, core], sibling)]
    for k in steps:
        for n, ring in enumerate((across, sibling_across)):
            tells.append(started(
                news, news_in.at[RING - k, core], news_send.at[k, n], news_recv.at[RING - k, core], ring(k)
            ))
    lines = pl.ds(pl.multiple_of(core * (HD // 2), HD // 2), HD // 2)
    out_lines = pl.ds(pl.multiple_of(3 * HD + core * (HD // 2), HD // 2), HD // 2)
    wouts = [
        started(weights.at[out_lines], wall.at[head, lines], wout_send.at[k], wout_recv.at[k], peer(k))
        for k in range(1, HEADS)
    ]

    for copy in w_copies:
        copy.wait()
    w_high, w_low = split(w_v[...])
    w_high, w_low = w_high.astype(BF16), w_low.astype(BF16)

    @pl.loop(0, OWN)
    def _(i):
        rows = pl.ds(pl.multiple_of(i * BLOCK, BLOCK), BLOCK)
        node_copy(i).wait()
        high, low = split(nodes_v[rows, :])
        high, low = high.astype(BF16), low.astype(BF16)
        out = nt(high, w_high) + nt(high, w_low) + nt(low, w_high)
        mine[0, i] = out[:HALF, :HALF]
        mine[1, i] = out[HALF:, :HALF]
        q_high, q_low = split(out[:, HALF:] * (1.0 / HD**0.5))
        qcat[rows, :HALF] = q_high.astype(BF16)
        qcat[rows, HALF:] = q_low.astype(BF16)

    def part(position, chunk):
        return grp.at[pl.ds(position * CHIP + chunk * OWN, OWN)]

    to_sibling = started(mine.at[other], part(there, core), sib_send, sib_recv, sibling)
    def send(way, chunk):
        src = mine.at[core] if chunk == 0 else part(here, other)
        place_there = part(here, core if chunk == 0 else other)
        return started(src, place_there, ring_send.at[way, chunk], ring_recv.at[way, chunk], along((1, RING - 1)[way]))

    sends = {(0, 0): send(0, 0)}
    to_sibling.wait()
    for way, chunk in ((1, 1), (0, 1), (1, 0)):
        sends[way, chunk] = send(way, chunk)

    @pl.loop(0, OWN)
    def _(i):
        grp[here * CHIP + core * OWN + i] = mine[core, i]

    for k in range(RING):
        for c in (core, other) if k else (other,):
            remote(news, news_in.at[k, c], news_send.at[0, 0], news_recv.at[k, c], sibling).wait_recv()
    for copy in tells:
        copy.wait_send()
    home = jnp.zeros((8, BLOCKS), I32)
    used = jnp.zeros((8, BLOCKS), F32)
    for k in range(RING):
        chip = jnp.maximum(news[...], news_in[0, other]) if k == 0 else jnp.maximum(news_in[k, 0], news_in[k, 1])
        for half, at in enumerate((lax.rem(y + k * other, RING), lax.rem(x + k * core, RING))):
            used = jnp.where(line == 2 * k + half, chip[half : half + 1, :], used)
            home = jnp.where(line == 2 * k + half, at, home)
    i, j = lax.broadcasted_iota(I32, (BLOCKS, BLOCKS), 0), lane((BLOCKS, BLOCKS))
    earlier = jnp.where((i < j) & ((i >> 6) == (j >> 6)), 1.0, 0.0).astype(BF16)
    ranks = jnp.dot(used.astype(BF16), earlier, preferred_element_type=F32)
    filled = jnp.where((used > 0.5) & ((lane((8, BLOCKS)) >> 6) != home), ranks + 1.0, 0.0)
    top = jnp.max(jnp.max(filled, axis=0, keepdims=True), axis=1, keepdims=True)
    most[...] = jnp.broadcast_to(top, (8, HALF))
    tell_most = [
        started(most, most_in.at[RING - k], most_send.at[k], most_recv.at[RING - k], along(k)) for k in steps
    ]
    result = jnp.zeros((NEEDS, HALF), F32)
    for half in range(2):
        rank = jnp.zeros((NEEDS, 1), F32)
        for n in range(BLOCKS // HALF):
            row = ranks[half : half + 1, n * HALF : (n + 1) * HALF]
            rank += jnp.sum(jnp.where(wanted[half] == column + n * HALF, row, 0.0), axis=1, keepdims=True)
        away = ((wanted[half] >> 6) + RING - (y if half == 0 else x)) & 3
        slot = jnp.where(away == 0, (wanted[half] & 63).astype(F32), (GROUP + (away - 1) * STRIDE).astype(F32) + rank)
        result = jnp.where(column == SPOT + half, slot, result)
        result = jnp.where(column == PLACE + half, wanted[half].astype(F32), result)
    ids = lane((1, BLOCKS))
    slot = lax.broadcasted_iota(I32, (NEEDS, BLOCKS), 0).astype(F32)
    for k in steps:
        use, rank = (
            jnp.where(core == 0, both[2 * k : 2 * k + 1, :], both[2 * k + 1 : 2 * k + 2, :]) for both in (used, ranks)
        )
        rank = jnp.where((use > 0.5) & ((ids >> 6) == there), rank, -1.0)
        pick = jnp.sum(jnp.where(rank == slot, (ids & 63).astype(F32), 0.0), axis=1, keepdims=True)
        result = jnp.where(column == PICK + k, pick, result)

    sends[0, 0].wait_recv()
    on = started(part(before, core), part(before, core), pass_send.at[0], pass_recv.at[0], along(1))
    sends[1, 1].wait_recv()
    back = started(part(after, other), part(after, other), pass_send.at[1], pass_recv.at[1], along(RING - 1))
    shares = []
    for k in range(1, HEADS):
        wouts[k - 1].wait()
        spot = wall.at[lax.rem(head + HEADS - k, HEADS), lines]
        shares.append(started(spot, spot, share_send.at[k], share_recv.at[k], sibling))
    for copy in tell_most:
        copy.wait()
    top = most[...]
    for k in steps:
        top = jnp.maximum(top, most_in[k])
    top = top[0:1, :]
    level = sum(jnp.where(top > slots, 1.0, 0.0) for slots in SLOTS)
    result = jnp.where(column == LEVEL, level, result)
    table[...] = result.astype(I32)

    sends[0, 1].wait_recv()
    sends[1, 0].wait_recv()
    on.wait_recv()
    back.wait_recv()
    wout_copy.wait()
    for copy in shares:
        copy.wait()
    for copy in sends.values():
        copy.wait_send()
    on.wait_send()
    back.wait_send()


def prepare(nodes_v, wall, w_high, w_low, nodes_t):
    high, low = split(wall[...].reshape(HEADS * HD, HEADS * HD).T)
    w_high[...] = high.astype(BF16)
    w_low[...] = low.astype(BF16)
    nodes_t[...] = nodes_v[...].T


def finish(
    table, base, qcat, updated, log_sums, held, mask_v, w_high, w_low, nodes_t,
    score, sums, attended, arrived, columns, a_send, a_recv, b_send, b_recv,
):
    head = lax.axis_index("head")
    lanes = lane((HALF, HALF)) < HD

    def a_copy(offset):
        return remote(attended.at[offset], arrived.at[head], a_send.at[offset], a_recv.at[offset], peer(offset))

    @pl.loop(0, OWN)
    def _(s):
        odd = lax.rem(s, 2)
        offset = 4 + lax.div(s, 2) * (1 - odd) - lax.div(s + 1, 2) * odd
        row = lax.rem(head + offset, HEADS)
        rows = pl.ds(pl.multiple_of(row * BLOCK, BLOCK), BLOCK)
        query = qcat[rows, :]
        values = []
        for t in range(TILES):
            for half in range(2):
                high, low = split(held[half, table[row * TILES + t, base + half]])
                keys = jnp.where(lanes, high, turned(low)).astype(BF16)
                values.append(jnp.where(lanes, turned(high), low).astype(BF16))
                found = nt(query, jnp.concatenate([keys, keys], axis=1))
                live = mask_v[row, t, :, half * HALF : (half + 1) * HALF] != 0
                if t == 0:
                    i = lax.broadcasted_iota(I32, (BLOCK, HALF), 0)
                    live = live | (i == lane((BLOCK, HALF)) + half * HALF)
                n = t * 2 + half
                score[:, n * HALF : (n + 1) * HALF] = jnp.where(live, found, -1e30)
        top = jnp.max(score[...], axis=1, keepdims=True)
        weights = jnp.exp(score[...] - top)
        total = jnp.sum(weights, axis=1, keepdims=True)
        high = weights.astype(BF16)
        low = (weights - high.astype(F32)).astype(BF16)
        value = jnp.concatenate(values, axis=0)
        both = jnp.dot(high, value, preferred_element_type=F32) + jnp.dot(low, value, preferred_element_type=F32)
        result = (both + turned(both)) / total
        sums[...] = jnp.where(lane((BLOCK, HALF)) == row, top + jnp.log(total), sums[...])
        packed = jnp.where(lanes, result[:HALF], result[HALF:])

        @pl.when(offset != 0)
        def _():
            attended[offset] = packed
            a_copy(offset).start()

        @pl.when(offset == 0)
        def _():
            arrived[head] = packed

    for k in range(1, HEADS):
        a_copy(k).wait()
    merged = []
    for pair in range(HEADS // 2):
        one, two = arrived[2 * pair], arrived[2 * pair + 1]
        merged.append(jnp.concatenate([jnp.where(lanes, one, turned(two)), jnp.where(lanes, turned(one), two)], axis=0))
    m_high, m_low = split(jnp.concatenate(merged, axis=1))
    m_high, m_low = m_high.astype(BF16), m_low.astype(BF16)
    columns[...] = nodes_t[...] + (nt(w_high[...], m_high) + nt(w_low[...], m_high) + nt(w_high[...], m_low))
    mine = pl.ds(pl.multiple_of(head * BLOCK, BLOCK), BLOCK)
    finals = []
    for k in range(1, HEADS):
        rows = pl.ds(pl.multiple_of(lax.rem(head + k, HEADS) * HD, HD), HD)
        finals.append(started(columns.at[rows], updated.at[:, mine], b_send.at[k], b_recv.at[k], peer(k)))
    updated[:, mine] = columns[pl.ds(pl.multiple_of(head * HD, HD), HD), :]
    flat = sums[...].T
    for row in range(OWN):
        log_sums[:, row * BLOCK : (row + 1) * BLOCK] = flat[row : row + 1, :]
    for send in finals:
        send.wait()


def fetch(nodes, masks, node_v, mask_v, node_sem, mask_sem):
    start = pl.multiple_of(lax.axis_index("head") * BLOCK, BLOCK)
    node_copy = pltpu.make_async_copy(nodes.at[pl.ds(start, BLOCK)], node_v, node_sem)
    node_copy.start()
    mask_copy = pltpu.make_async_copy(masks, mask_v, mask_sem)
    mask_copy.start()
    return node_copy, mask_copy


def picked_kernel(
    slots, table, grp, qcat, wall, nodes, masks, updated, log_sums,
    held, packets, mask_v, node_v, w_high, w_low, nodes_t, score, sums, attended, arrived, columns,
    mask_sem, node_sem, own_send, own_recv, ring_send, ring_recv,
    sib_send, sib_recv, a_send, a_recv, b_send, b_recv,
):
    x, y, core = place()
    sibling = device(x, y, 1 - core)
    along, _ = second_axis(x, y, core)
    steps = (2, 1, 3)
    friends = [sibling] + [along(k) for k in steps] + [peer(k) for k in range(1, HEADS)]
    greet(friends)
    node_copy, mask_copy = fetch(nodes, masks, node_v, mask_v, node_sem, mask_sem)
    part = slots // 2

    def fill(k):
        @pl.loop(0, slots)
        def _(s):
            packets[k, s] = grp[table[s, PICK + k]]

    def spot(away, chunk):
        return held.at[core, pl.ds(GROUP + (away - 1) * STRIDE + chunk * part, part)]

    for step in steps:
        fill(step)
    met(len(friends))
    sends = [
        (step, chunk, started(
            packets.at[step, pl.ds(chunk * part, part)], spot(RING - step, chunk),
            ring_send.at[step, chunk], ring_recv.at[step, chunk], along(step),
        ))
        for chunk in range(2)
        for step in steps
    ]
    own = started(grp, held.at[core, pl.ds(0, GROUP)], own_send, own_recv, sibling)

    @pl.loop(0, GROUP)
    def _(i):
        held[core, i] = grp[i]

    sums[...] = jnp.zeros_like(sums)
    node_copy.wait()
    prepare(node_v, wall, w_high, w_low, nodes_t)

    forwards = []
    for n, (step, chunk, send) in enumerate(sends):
        send.wait_recv()
        one = spot(RING - step, chunk)
        forwards.append(started(one, one, sib_send.at[n], sib_recv.at[n], sibling))
    mask_copy.wait()
    own.wait()
    for send in forwards:
        send.wait()
    for _, _, send in sends:
        send.wait_send()
    finish(
        table, SPOT, qcat, updated, log_sums, held, mask_v, w_high, w_low, nodes_t,
        score, sums, attended, arrived, columns, a_send, a_recv, b_send, b_recv,
    )


def whole_kernel(
    table, grp, qcat, wall, nodes, masks, updated, log_sums,
    held, mask_v, node_v, w_high, w_low, nodes_t, score, sums, attended, arrived, columns,
    mask_sem, node_sem, own_send, own_recv, ring_send, ring_recv, pass_send, pass_recv,
    sib_send, sib_recv, a_send, a_recv, b_send, b_recv,
):
    x, y, core = place()
    sibling = device(x, y, 1 - core)
    along, here = second_axis(x, y, core)
    before, after, far = (lax.rem(here + k, RING) for k in (RING - 1, 1, 2))
    ways = (1, RING - 1)
    friends = [sibling, along(1), along(RING - 1)] + [peer(k) for k in range(1, HEADS)]
    greet(friends)
    node_copy, mask_copy = fetch(nodes, masks, node_v, mask_v, node_sem, mask_sem)
    met(len(friends))

    def spot(position, p, chunk):
        return held.at[core, pl.ds((position * RING + p) * CHIP + chunk * OWN, OWN)]

    sends = {}
    for p in range(RING):
        for chunk in range(2):
            for way, step in enumerate(ways):
                part = chunk if way == 0 else 1 - chunk
                sends[way, p, part] = started(
                    grp.at[pl.ds(p * CHIP + part * OWN, OWN)], spot(here, p, part),
                    ring_send.at[way, p, part], ring_recv.at[way, p, part], along(step),
                )
    own = started(grp, held.at[core, pl.ds(here * GROUP, GROUP)], own_send, own_recv, sibling)

    @pl.loop(0, GROUP)
    def _(i):
        held[core, here * GROUP + i] = grp[i]

    sums[...] = jnp.zeros_like(sums)
    node_copy.wait()
    prepare(node_v, wall, w_high, w_low, nodes_t)
    forwards = []
    passes = []

    def forward(position, p, chunk):
        n = len(forwards)
        one = spot(position, p, chunk)
        forwards.append(started(one, one, sib_send.at[n], sib_recv.at[n], sibling))

    for chunk in range(2):
        for p in range(RING):
            for way, step in enumerate(ways):
                part = chunk if way == 0 else 1 - chunk
                origin = before if way == 0 else after
                sends[way, p, part].wait_recv()
                if chunk == 0:
                    one = spot(origin, p, part)
                    passes.append((started(one, one, pass_send.at[way, p], pass_recv.at[way, p], along(step)), p, part))
                forward(origin, p, part)
    for send, p, part in passes:
        send.wait_recv()
        forward(far, p, part)
    mask_copy.wait()
    own.wait()
    for send in forwards:
        send.wait()
    for send in sends.values():
        send.wait_send()
    for send, _, _ in passes:
        send.wait_send()
    finish(
        table, PLACE, qcat, updated, log_sums, held, mask_v, w_high, w_low, nodes_t,
        score, sums, attended, arrived, columns, a_send, a_recv, b_send, b_recv,
    )


def body(nodes, w_query, w_key, w_value, w_out, tile_cols, tile_masks):
    vmem = pl.BlockSpec(memory_space=pltpu.VMEM)
    smem = pl.BlockSpec(memory_space=pltpu.SMEM)
    hbm = pl.BlockSpec(memory_space=pl.ANY)
    far = pl.BlockSpec(memory_space=pltpu.HBM)
    dma = pltpu.SemaphoreType.DMA
    rows = nodes.shape[0]
    scratch = pltpu.VMEM
    asked = jnp.broadcast_to(tile_cols.reshape(NEEDS, 1), (NEEDS, HALF))
    weights = jnp.concatenate([w_key.T, w_value.T, w_query.T, w_out], axis=0)
    grp, qcat, wall, table = pl.pallas_call(
        project_kernel,
        out_shape=(
            jax.ShapeDtypeStruct((GROUP, HALF, HALF), F32),
            jax.ShapeDtypeStruct((rows, 2 * HALF), BF16),
            jax.ShapeDtypeStruct((HEADS, HD, HEADS * HD), F32),
            jax.ShapeDtypeStruct((NEEDS, HALF), I32),
        ),
        in_specs=[far, far, vmem],
        out_specs=(vmem,) * 4,
        scratch_shapes=[
            scratch((rows, HEADS * HD), F32), scratch((4 * HD, HEADS * HD), F32),
            scratch((2, OWN, HALF, HALF), F32),
            scratch((8, BLOCKS), F32), scratch((RING, 2, 8, BLOCKS), F32),
            scratch((8, HALF), F32), scratch((RING, 8, HALF), F32),
            dma((OWN,)), dma((3,)),
            dma((2, 2)), dma((2, 2)), dma((2,)), dma((2,)), dma, dma,
            dma((RING, 2)), dma((RING, 2)), dma((RING,)), dma((RING,)),
            dma((HEADS,)), dma((HEADS,)), dma((HEADS,)), dma((HEADS,)),
        ],
        compiler_params=pltpu.CompilerParams(collective_id=0, has_side_effects=True, vmem_limit_bytes=24 * 2**20),
        name="project",
    )(nodes, weights, asked)

    def second(kernel, name, number, slots, extra, semaphores, limit):
        def call(*operands):
            return pl.pallas_call(
                kernel,
                out_shape=(jax.ShapeDtypeStruct((HD, rows), F32), jax.ShapeDtypeStruct((1, rows), F32)),
                in_specs=[smem, vmem, vmem, vmem, hbm, hbm],
                out_specs=(vmem, vmem),
                scratch_shapes=[
                    scratch((2, slots, HALF, HALF), F32),
                    *extra,
                    scratch((OWN, TILES, BLOCK, BLOCK), I32),
                    scratch((BLOCK, HEADS * HD), F32),
                    scratch((HEADS * HD, HEADS * HD), BF16), scratch((HEADS * HD, HEADS * HD), BF16),
                    scratch((HEADS * HD, BLOCK), F32),
                    scratch((BLOCK, TILES * BLOCK), F32),
                    scratch((BLOCK, HALF), F32),
                    scratch((HEADS, HALF, HALF), F32), scratch((HEADS, HALF, HALF), F32),
                    scratch((HEADS * HD, BLOCK), F32),
                    dma, dma, dma, dma,
                    *semaphores,
                    dma((HEADS,)), dma((HEADS,)), dma((HEADS,)), dma((HEADS,)),
                ],
                compiler_params=pltpu.CompilerParams(
                    collective_id=number, has_side_effects=True, vmem_limit_bytes=limit * 2**20
                ),
                name=name,
            )(*operands)

        return call

    branches = [
        second(
            functools.partial(picked_kernel, slots), f"picked_{slots}", 1 + n, GROUP + 3 * STRIDE,
            [scratch((RING, slots, HALF, HALF), F32)],
            [dma((RING, 2)), dma((RING, 2)), dma((6,)), dma((6,))],
            40,
        )
        for n, slots in enumerate(SLOTS)
    ]
    branches.append(second(
        whole_kernel, "whole", 1 + len(SLOTS), BLOCKS, [],
        [dma((2, RING, 2)), dma((2, RING, 2)), dma((2, RING)), dma((2, RING)), dma((24,)), dma((24,))],
        48,
    ))
    updated, log_sums = lax.switch(
        table[0, LEVEL], branches, table, grp, qcat, wall, nodes, tile_masks
    )
    return updated.T, log_sums.T


def solution(mesh):
    placed = (
        P(("replica", "blk"), None),
        P(None, "head"),
        P(None, "head"),
        P(None, "head"),
        P("head", None),
        P(("replica", "blk"), None),
        P(("replica", "blk"), None, None, None),
    )
    return jax.shard_map(
        body,
        mesh=mesh,
        in_specs=placed,
        out_specs=(P(("replica", "blk"), "head"), P(("replica", "blk"), "head")),
        check_vma=False,
    )
```

```python
import functools

import jax
import jax.numpy as jnp
from jax import lax
from jax.experimental import pallas as pl
from jax.experimental.pallas import tpu as pltpu
from jax.sharding import PartitionSpec as P

MESH = pl.DeviceIdType.MESH
F32 = jnp.float32
BF16 = jnp.bfloat16
I32 = jnp.int32

HEADS = 8
HD = 64
BLOCK = 256
HALF = 128
TILES = 4
OWN = 8
CHIP = 16
RING = 4
GROUP = RING * CHIP
BLOCKS = RING * GROUP
SLOTS = (18, 20, 24)
STRIDE = SLOTS[-1]
NEEDS = OWN * TILES
PICK, SPOT, PLACE, LEVEL = 0, 8, 16, 24


def place():
    replica, blk = lax.axis_index("replica"), lax.axis_index("blk")
    core = lax.rem(blk, 2)
    x = lax.rem(lax.div(blk, 2), 2) * 2 + replica
    y = lax.div(blk, 4)
    return x, y, core


def device(x, y, core):
    return {"replica": lax.rem(x, 2), "blk": (y * 2 + lax.div(x, 2)) * 2 + core}


def first_axis(x, y, core):
    def along(step):
        return device(lax.rem(x + step * (1 - core), RING), lax.rem(y + step * core, RING), core)

    return along, x * (1 - core) + y * core


def second_axis(x, y, core):
    def along(step):
        return device(lax.rem(x + step * core, RING), lax.rem(y + step * (1 - core), RING), core)

    return along, x * core + y * (1 - core)


def peer(step):
    return {"head": lax.rem(lax.axis_index("head") + step, HEADS)}


def split(value):
    high = value.astype(BF16).astype(F32)
    return high, value - high


def turned(value):
    return pltpu.roll(value, HD, 1)


def nt(a, b):
    return lax.dot_general(a, b, (((1,), (1,)), ((), ())), preferred_element_type=F32)


def lane(shape):
    return lax.broadcasted_iota(I32, shape, 1)


def greet(devices):
    for one in devices:
        pl.semaphore_signal(pltpu.get_barrier_semaphore(), inc=1, device_id=one, device_id_type=MESH)


def met(count):
    pl.semaphore_wait(pltpu.get_barrier_semaphore(), count)


def remote(src, dst, send, recv, to):
    return pltpu.make_async_remote_copy(
        src_ref=src, dst_ref=dst, send_sem=send, recv_sem=recv, device_id=to, device_id_type=MESH
    )


def started(*what):
    copy = remote(*what)
    copy.start()
    return copy


def project_kernel(
    nodes, weights, asked, grp, qcat, wall, table,
    nodes_v, w_v, mine, news, news_in, most, most_in,
    node_sem, w_sem, ring_send, ring_recv, pass_send, pass_recv, sib_send, sib_recv,
    news_send, news_recv, most_send, most_recv, wout_send, wout_recv, share_send, share_recv,
):
    x, y, core = place()
    head = lax.axis_index("head")
    other = 1 - core
    sibling = device(x, y, other)
    along, here = first_axis(x, y, core)
    across, there = second_axis(x, y, core)
    sibling_across, _ = second_axis(x, y, other)
    sibling_along, _ = first_axis(x, y, other)
    before, after = lax.rem(here + RING - 1, RING), lax.rem(here + 1, RING)
    steps = (1, 2, 3)
    friends = [sibling] + [peer(k) for k in range(1, HEADS)]
    for ring in (along, across, sibling_across, sibling_along):
        friends += [ring(k) for k in steps]
    greet(friends)
    w_copies = [
        pltpu.make_async_copy(weights.at[pl.ds(0, 3 * HD)], w_v.at[pl.ds(0, 3 * HD)], w_sem.at[0]),
        pltpu.make_async_copy(weights.at[pl.ds(2 * HD, HD)], w_v.at[pl.ds(3 * HD, HD)], w_sem.at[1]),
    ]
    for copy in w_copies:
        copy.start()

    def node_copy(i):
        rows = pl.ds(pl.multiple_of(i * BLOCK, BLOCK), BLOCK)
        return pltpu.make_async_copy(nodes.at[rows], nodes_v.at[rows], node_sem.at[i])

    for i in range(OWN):
        node_copy(i).start()
    wout_copy = pltpu.make_async_copy(weights.at[pl.ds(3 * HD, HD)], wall.at[head], w_sem.at[2])
    wout_copy.start()

    def positions(col):
        replica, blk, i = col >> 7, (col >> 3) & 15, col & 7
        px, py, pc = ((blk >> 1) & 1) * 2 + replica, blk >> 2, blk & 1
        return (py * RING + px) * CHIP + pc * OWN + i, (px * RING + py) * CHIP + pc * OWN + i

    column = lane((NEEDS, HALF))
    wanted = positions(asked[...])
    line = lax.broadcasted_iota(I32, (8, BLOCKS), 0)
    used = jnp.zeros((8, BLOCKS), F32)
    for half in range(2):
        hits = [jnp.where(wanted[half] == column + n * HALF, 1.0, 0.0) for n in range(BLOCKS // HALF)]
        row = jnp.concatenate([jnp.max(one, axis=0, keepdims=True) for one in hits], axis=1)
        used = jnp.where(line == half, row, used)
    news[...] = used
    met(len(friends))
    tells = [started(news, news_in.at[0, core], news_send.at[0, 0], news_recv.at[0, core], sibling)]
    for k in steps:
        for n, ring in enumerate((across, sibling_across)):
            tells.append(started(
                news, news_in.at[RING - k, core], news_send.at[k, n], news_recv.at[RING - k, core], ring(k)
            ))
    for copy in w_copies:
        copy.wait()
    w_high, w_low = split(w_v[...])
    w_high, w_low = w_high.astype(BF16), w_low.astype(BF16)

    @pl.loop(0, OWN)
    def _(i):
        rows = pl.ds(pl.multiple_of(i * BLOCK, BLOCK), BLOCK)
        node_copy(i).wait()
        high, low = split(nodes_v[rows, :])
        high, low = high.astype(BF16), low.astype(BF16)
        out = nt(high, w_high) + nt(high, w_low) + nt(low, w_high)
        mine[0, i] = out[:HALF, :HALF]
        mine[1, i] = out[HALF:, :HALF]
        q_high, q_low = split(out[:, HALF:] * (1.0 / HD**0.5))
        qcat[rows, :HALF] = q_high.astype(BF16)
        qcat[rows, HALF:] = q_low.astype(BF16)

    def part(position, chunk):
        return grp.at[pl.ds(position * CHIP + chunk * OWN, OWN)]

    to_sibling = started(mine.at[other], part(there, core), sib_send, sib_recv, sibling)
    def send(way, chunk):
        src = mine.at[core] if chunk == 0 else part(here, other)
        place_there = part(here, core if chunk == 0 else other)
        return started(src, place_there, ring_send.at[way, chunk], ring_recv.at[way, chunk], along((1, RING - 1)[way]))

    sends = {(0, 0): send(0, 0)}
    to_sibling.wait()
    for way, chunk in ((1, 1), (0, 1), (1, 0)):
        sends[way, chunk] = send(way, chunk)

    lines = pl.ds(pl.multiple_of(core * (HD // 2), HD // 2), HD // 2)
    out_lines = pl.ds(pl.multiple_of(3 * HD + core * (HD // 2), HD // 2), HD // 2)
    wouts = [
        started(weights.at[out_lines], wall.at[head, lines], wout_send.at[k], wout_recv.at[k], peer(k))
        for k in range(1, HEADS)
    ]

    @pl.loop(0, OWN)
    def _(i):
        grp[here * CHIP + core * OWN + i] = mine[core, i]

    for k in range(RING):
        for c in (core, other) if k else (other,):
            remote(news, news_in.at[k, c], news_send.at[0, 0], news_recv.at[k, c], sibling).wait_recv()
    for copy in tells:
        copy.wait_send()
    home = jnp.zeros((8, BLOCKS), I32)
    used = jnp.zeros((8, BLOCKS), F32)
    for k in range(RING):
        chip = jnp.maximum(news[...], news_in[0, other]) if k == 0 else jnp.maximum(news_in[k, 0], news_in[k, 1])
        for half, at in enumerate((lax.rem(y + k * other, RING), lax.rem(x + k * core, RING))):
            used = jnp.where(line == 2 * k + half, chip[half : half + 1, :], used)
            home = jnp.where(line == 2 * k + half, at, home)
    i, j = lax.broadcasted_iota(I32, (BLOCKS, BLOCKS), 0), lane((BLOCKS, BLOCKS))
    earlier = jnp.where((i < j) & ((i >> 6) == (j >> 6)), 1.0, 0.0).astype(BF16)
    ranks = jnp.dot(used.astype(BF16), earlier, preferred_element_type=F32)
    filled = jnp.where((used > 0.5) & ((lane((8, BLOCKS)) >> 6) != home), ranks + 1.0, 0.0)
    top = jnp.max(jnp.max(filled, axis=0, keepdims=True), axis=1, keepdims=True)
    most[...] = jnp.broadcast_to(top, (8, HALF))
    tell_most = [
        started(most, most_in.at[RING - k], most_send.at[k], most_recv.at[RING - k], along(k)) for k in steps
    ]
    result = jnp.zeros((NEEDS, HALF), F32)
    for half in range(2):
        rank = jnp.zeros((NEEDS, 1), F32)
        for n in range(BLOCKS // HALF):
            row = ranks[half : half + 1, n * HALF : (n + 1) * HALF]
            rank += jnp.sum(jnp.where(wanted[half] == column + n * HALF, row, 0.0), axis=1, keepdims=True)
        away = ((wanted[half] >> 6) + RING - (y if half == 0 else x)) & 3
        slot = jnp.where(away == 0, (wanted[half] & 63).astype(F32), (GROUP + (away - 1) * STRIDE).astype(F32) + rank)
        result = jnp.where(column == SPOT + half, slot, result)
        result = jnp.where(column == PLACE + half, wanted[half].astype(F32), result)
    ids = lane((1, BLOCKS))
    slot = lax.broadcasted_iota(I32, (NEEDS, BLOCKS), 0).astype(F32)
    for k in steps:
        use, rank = (
            jnp.where(core == 0, both[2 * k : 2 * k + 1, :], both[2 * k + 1 : 2 * k + 2, :]) for both in (used, ranks)
        )
        rank = jnp.where((use > 0.5) & ((ids >> 6) == there), rank, -1.0)
        pick = jnp.sum(jnp.where(rank == slot, (ids & 63).astype(F32), 0.0), axis=1, keepdims=True)
        result = jnp.where(column == PICK + k, pick, result)

    sends[0, 0].wait_recv()
    on = started(part(before, core), part(before, core), pass_send.at[0], pass_recv.at[0], along(1))
    sends[1, 1].wait_recv()
    back = started(part(after, other), part(after, other), pass_send.at[1], pass_recv.at[1], along(RING - 1))
    shares = []
    for k in range(1, HEADS):
        wouts[k - 1].wait()
        spot = wall.at[lax.rem(head + HEADS - k, HEADS), lines]
        shares.append(started(spot, spot, share_send.at[k], share_recv.at[k], sibling))
    for copy in tell_most:
        copy.wait()
    top = most[...]
    for k in steps:
        top = jnp.maximum(top, most_in[k])
    top = top[0:1, :]
    level = sum(jnp.where(top > slots, 1.0, 0.0) for slots in SLOTS)
    result = jnp.where(column == LEVEL, level, result)
    table[...] = result.astype(I32)

    sends[0, 1].wait_recv()
    sends[1, 0].wait_recv()
    on.wait_recv()
    back.wait_recv()
    wout_copy.wait()
    for copy in shares:
        copy.wait()
    for copy in sends.values():
        copy.wait_send()
    on.wait_send()
    back.wait_send()


def prepare(nodes_v, wall, w_high, w_low, nodes_t):
    high, low = split(wall[...].reshape(HEADS * HD, HEADS * HD).T)
    w_high[...] = high.astype(BF16)
    w_low[...] = low.astype(BF16)
    nodes_t[...] = nodes_v[...].T


def finish(
    table, base, qcat, updated, log_sums, held, mask_v, w_high, w_low, nodes_t,
    score, sums, attended, arrived, columns, a_send, a_recv, b_send, b_recv,
):
    head = lax.axis_index("head")
    lanes = lane((HALF, HALF)) < HD

    def a_copy(offset):
        return remote(attended.at[offset], arrived.at[head], a_send.at[offset], a_recv.at[offset], peer(offset))

    @pl.loop(0, OWN)
    def _(s):
        odd = lax.rem(s, 2)
        offset = 4 + lax.div(s, 2) * (1 - odd) - lax.div(s + 1, 2) * odd
        row = lax.rem(head + offset, HEADS)
        rows = pl.ds(pl.multiple_of(row * BLOCK, BLOCK), BLOCK)
        query = qcat[rows, :]
        values = []
        for t in range(TILES):
            for half in range(2):
                high, low = split(held[half, table[row * TILES + t, base + half]])
                keys = jnp.where(lanes, high, turned(low)).astype(BF16)
                values.append(jnp.where(lanes, turned(high), low).astype(BF16))
                found = nt(query, jnp.concatenate([keys, keys], axis=1))
                live = mask_v[row, t, :, half * HALF : (half + 1) * HALF] != 0
                if t == 0:
                    i = lax.broadcasted_iota(I32, (BLOCK, HALF), 0)
                    live = live | (i == lane((BLOCK, HALF)) + half * HALF)
                n = t * 2 + half
                score[:, n * HALF : (n + 1) * HALF] = jnp.where(live, found, -1e30)
        top = jnp.max(score[...], axis=1, keepdims=True)
        weights = jnp.exp(score[...] - top)
        total = jnp.sum(weights, axis=1, keepdims=True)
        high = weights.astype(BF16)
        low = (weights - high.astype(F32)).astype(BF16)
        value = jnp.concatenate(values, axis=0)
        both = jnp.dot(high, value, preferred_element_type=F32) + jnp.dot(low, value, preferred_element_type=F32)
        result = (both + turned(both)) / total
        sums[...] = jnp.where(lane((BLOCK, HALF)) == row, top + jnp.log(total), sums[...])
        packed = jnp.where(lanes, result[:HALF], result[HALF:])

        @pl.when(offset != 0)
        def _():
            attended[offset] = packed
            a_copy(offset).start()

        @pl.when(offset == 0)
        def _():
            arrived[head] = packed

    for k in range(1, HEADS):
        a_copy(k).wait()
    merged = []
    for pair in range(HEADS // 2):
        one, two = arrived[2 * pair], arrived[2 * pair + 1]
        merged.append(jnp.concatenate([jnp.where(lanes, one, turned(two)), jnp.where(lanes, turned(one), two)], axis=0))
    m_high, m_low = split(jnp.concatenate(merged, axis=1))
    m_high, m_low = m_high.astype(BF16), m_low.astype(BF16)
    columns[...] = nodes_t[...] + (nt(w_high[...], m_high) + nt(w_low[...], m_high) + nt(w_high[...], m_low))
    mine = pl.ds(pl.multiple_of(head * BLOCK, BLOCK), BLOCK)
    finals = []
    for k in (4, 3, 5, 2, 6, 1, 7):
        rows = pl.ds(pl.multiple_of(lax.rem(head + k, HEADS) * HD, HD), HD)
        finals.append(started(columns.at[rows], updated.at[:, mine], b_send.at[k], b_recv.at[k], peer(k)))
    updated[:, mine] = columns[pl.ds(pl.multiple_of(head * HD, HD), HD), :]
    flat = sums[...].T
    for row in range(OWN):
        log_sums[:, row * BLOCK : (row + 1) * BLOCK] = flat[row : row + 1, :]
    for send in finals:
        send.wait()


def fetch(nodes, masks, node_v, mask_v, node_sem, mask_sem):
    start = pl.multiple_of(lax.axis_index("head") * BLOCK, BLOCK)
    node_copy = pltpu.make_async_copy(nodes.at[pl.ds(start, BLOCK)], node_v, node_sem)
    node_copy.start()
    mask_copy = pltpu.make_async_copy(masks, mask_v, mask_sem)
    mask_copy.start()
    return node_copy, mask_copy


def picked_kernel(
    slots, table, grp, qcat, wall, nodes, masks, updated, log_sums,
    held, packets, mask_v, node_v, w_high, w_low, nodes_t, score, sums, attended, arrived, columns,
    mask_sem, node_sem, own_send, own_recv, ring_send, ring_recv,
    sib_send, sib_recv, a_send, a_recv, b_send, b_recv,
):
    x, y, core = place()
    sibling = device(x, y, 1 - core)
    along, _ = second_axis(x, y, core)
    steps = (2, 1, 3)
    friends = [sibling] + [along(k) for k in steps] + [peer(k) for k in range(1, HEADS)]
    greet(friends)
    node_copy, mask_copy = fetch(nodes, masks, node_v, mask_v, node_sem, mask_sem)
    part = slots // 2

    def fill(k):
        @pl.loop(0, slots)
        def _(s):
            packets[k, s] = grp[table[s, PICK + k]]

    def spot(away, chunk):
        return held.at[core, pl.ds(GROUP + (away - 1) * STRIDE + chunk * part, part)]

    for step in steps:
        fill(step)
    met(len(friends))
    sends = [
        (step, chunk, started(
            packets.at[step, pl.ds(chunk * part, part)], spot(RING - step, chunk),
            ring_send.at[step, chunk], ring_recv.at[step, chunk], along(step),
        ))
        for chunk in range(2)
        for step in steps
    ]
    own = started(grp, held.at[core, pl.ds(0, GROUP)], own_send, own_recv, sibling)

    @pl.loop(0, GROUP)
    def _(i):
        held[core, i] = grp[i]

    sums[...] = jnp.zeros_like(sums)
    node_copy.wait()
    prepare(node_v, wall, w_high, w_low, nodes_t)

    forwards = []
    for n, (step, chunk, send) in enumerate(sends):
        send.wait_recv()
        one = spot(RING - step, chunk)
        forwards.append(started(one, one, sib_send.at[n], sib_recv.at[n], sibling))
    mask_copy.wait()
    own.wait()
    for send in forwards:
        send.wait()
    for _, _, send in sends:
        send.wait_send()
    finish(
        table, SPOT, qcat, updated, log_sums, held, mask_v, w_high, w_low, nodes_t,
        score, sums, attended, arrived, columns, a_send, a_recv, b_send, b_recv,
    )


def whole_kernel(
    table, grp, qcat, wall, nodes, masks, updated, log_sums,
    held, mask_v, node_v, w_high, w_low, nodes_t, score, sums, attended, arrived, columns,
    mask_sem, node_sem, own_send, own_recv, ring_send, ring_recv, pass_send, pass_recv,
    sib_send, sib_recv, a_send, a_recv, b_send, b_recv,
):
    x, y, core = place()
    sibling = device(x, y, 1 - core)
    along, here = second_axis(x, y, core)
    before, after, far = (lax.rem(here + k, RING) for k in (RING - 1, 1, 2))
    ways = (1, RING - 1)
    friends = [sibling, along(1), along(RING - 1)] + [peer(k) for k in range(1, HEADS)]
    greet(friends)
    node_copy, mask_copy = fetch(nodes, masks, node_v, mask_v, node_sem, mask_sem)
    met(len(friends))

    def spot(position, p, chunk):
        return held.at[core, pl.ds((position * RING + p) * CHIP + chunk * OWN, OWN)]

    sends = {}
    for p in range(RING):
        for chunk in range(2):
            for way, step in enumerate(ways):
                part = chunk if way == 0 else 1 - chunk
                sends[way, p, part] = started(
                    grp.at[pl.ds(p * CHIP + part * OWN, OWN)], spot(here, p, part),
                    ring_send.at[way, p, part], ring_recv.at[way, p, part], along(step),
                )
    own = started(grp, held.at[core, pl.ds(here * GROUP, GROUP)], own_send, own_recv, sibling)

    @pl.loop(0, GROUP)
    def _(i):
        held[core, here * GROUP + i] = grp[i]

    sums[...] = jnp.zeros_like(sums)
    node_copy.wait()
    prepare(node_v, wall, w_high, w_low, nodes_t)
    forwards = []
    passes = []

    def forward(position, p, chunk):
        n = len(forwards)
        one = spot(position, p, chunk)
        forwards.append(started(one, one, sib_send.at[n], sib_recv.at[n], sibling))

    for chunk in range(2):
        for p in range(RING):
            for way, step in enumerate(ways):
                part = chunk if way == 0 else 1 - chunk
                origin = before if way == 0 else after
                sends[way, p, part].wait_recv()
                if chunk == 0:
                    one = spot(origin, p, part)
                    passes.append((started(one, one, pass_send.at[way, p], pass_recv.at[way, p], along(step)), p, part))
                forward(origin, p, part)
    for send, p, part in passes:
        send.wait_recv()
        forward(far, p, part)
    mask_copy.wait()
    own.wait()
    for send in forwards:
        send.wait()
    for send in sends.values():
        send.wait_send()
    for send, _, _ in passes:
        send.wait_send()
    finish(
        table, PLACE, qcat, updated, log_sums, held, mask_v, w_high, w_low, nodes_t,
        score, sums, attended, arrived, columns, a_send, a_recv, b_send, b_recv,
    )


def body(nodes, w_query, w_key, w_value, w_out, tile_cols, tile_masks):
    vmem = pl.BlockSpec(memory_space=pltpu.VMEM)
    smem = pl.BlockSpec(memory_space=pltpu.SMEM)
    hbm = pl.BlockSpec(memory_space=pl.ANY)
    far = pl.BlockSpec(memory_space=pltpu.HBM)
    dma = pltpu.SemaphoreType.DMA
    rows = nodes.shape[0]
    scratch = pltpu.VMEM
    asked = jnp.broadcast_to(tile_cols.reshape(NEEDS, 1), (NEEDS, HALF))
    weights = jnp.concatenate([w_key.T, w_value.T, w_query.T, w_out], axis=0)
    grp, qcat, wall, table = pl.pallas_call(
        project_kernel,
        out_shape=(
            jax.ShapeDtypeStruct((GROUP, HALF, HALF), F32),
            jax.ShapeDtypeStruct((rows, 2 * HALF), BF16),
            jax.ShapeDtypeStruct((HEADS, HD, HEADS * HD), F32),
            jax.ShapeDtypeStruct((NEEDS, HALF), I32),
        ),
        in_specs=[far, far, vmem],
        out_specs=(vmem,) * 4,
        scratch_shapes=[
            scratch((rows, HEADS * HD), F32), scratch((4 * HD, HEADS * HD), F32),
            scratch((2, OWN, HALF, HALF), F32),
            scratch((8, BLOCKS), F32), scratch((RING, 2, 8, BLOCKS), F32),
            scratch((8, HALF), F32), scratch((RING, 8, HALF), F32),
            dma((OWN,)), dma((3,)),
            dma((2, 2)), dma((2, 2)), dma((2,)), dma((2,)), dma, dma,
            dma((RING, 2)), dma((RING, 2)), dma((RING,)), dma((RING,)),
            dma((HEADS,)), dma((HEADS,)), dma((HEADS,)), dma((HEADS,)),
        ],
        compiler_params=pltpu.CompilerParams(collective_id=0, has_side_effects=True, vmem_limit_bytes=24 * 2**20),
        name="project",
    )(nodes, weights, asked)

    def second(kernel, name, number, slots, extra, semaphores, limit):
        def call(*operands):
            return pl.pallas_call(
                kernel,
                out_shape=(jax.ShapeDtypeStruct((HD, rows), F32), jax.ShapeDtypeStruct((1, rows), F32)),
                in_specs=[smem, vmem, vmem, vmem, hbm, hbm],
                out_specs=(vmem, vmem),
                scratch_shapes=[
                    scratch((2, slots, HALF, HALF), F32),
                    *extra,
                    scratch((OWN, TILES, BLOCK, BLOCK), I32),
                    scratch((BLOCK, HEADS * HD), F32),
                    scratch((HEADS * HD, HEADS * HD), BF16), scratch((HEADS * HD, HEADS * HD), BF16),
                    scratch((HEADS * HD, BLOCK), F32),
                    scratch((BLOCK, TILES * BLOCK), F32),
                    scratch((BLOCK, HALF), F32),
                    scratch((HEADS, HALF, HALF), F32), scratch((HEADS, HALF, HALF), F32),
                    scratch((HEADS * HD, BLOCK), F32),
                    dma, dma, dma, dma,
                    *semaphores,
                    dma((HEADS,)), dma((HEADS,)), dma((HEADS,)), dma((HEADS,)),
                ],
                compiler_params=pltpu.CompilerParams(
                    collective_id=number, has_side_effects=True, vmem_limit_bytes=limit * 2**20
                ),
                name=name,
            )(*operands)

        return call

    branches = [
        second(
            functools.partial(picked_kernel, slots), f"picked_{slots}", 1 + n, GROUP + 3 * STRIDE,
            [scratch((RING, slots, HALF, HALF), F32)],
            [dma((RING, 2)), dma((RING, 2)), dma((6,)), dma((6,))],
            40,
        )
        for n, slots in enumerate(SLOTS)
    ]
    branches.append(second(
        whole_kernel, "whole", 1 + len(SLOTS), BLOCKS, [],
        [dma((2, RING, 2)), dma((2, RING, 2)), dma((2, RING)), dma((2, RING)), dma((24,)), dma((24,))],
        48,
    ))
    updated, log_sums = lax.switch(
        table[0, LEVEL], branches, table, grp, qcat, wall, nodes, tile_masks
    )
    return updated.T, log_sums.T


def solution(mesh):
    placed = (
        P(("replica", "blk"), None),
        P(None, "head"),
        P(None, "head"),
        P(None, "head"),
        P("head", None),
        P(("replica", "blk"), None),
        P(("replica", "blk"), None, None, None),
    )
    return jax.shard_map(
        body,
        mesh=mesh,
        in_specs=placed,
        out_specs=(P(("replica", "blk"), "head"), P(("replica", "blk"), "head")),
        check_vma=False,
    )
```
